32 devices in a mesh: row: 16 (over z, y, core), col: 2 (over x).
Axes of the slice: x: 2, y: 2, z: 4, core: 2. Of those that a mesh axis runs over, the one named last changes fastest.
Arguments:
- left_blocks: bfloat16 [2, 2, 64, 4096], P('col', None, 'row'), may hold values from -0.75 to 0.75
- left_slots: int32 [2, 2, 64], P('col', None, 'row'), may hold values from 0 to 15, as said below
- left_lengths: int32 [2, 2, 8], P('col'), may hold values from 1 to 8, as said below
- right_blocks: bfloat16 [2, 16, 32, 4096], P('col', 'row'), may hold values from -6 to 6
- right_places: int32 [2, 16, 32], P('col', 'row'), may hold values from 0 to 255, as said below
- right_count: int32 [2, 16], P('col', 'row'), may hold values from 1 to 32, as said below
Outputs:
- product: float32 [1024, 16384], P('col', 'row')
The draws below stay inside these ranges and needn't reach their ends.
Inputs may be any that keep to these rules, and one draw needn't show every extreme that they name: `left_slots`: within one block-row of one left tile the 8 slots name distinct block-columns. `left_lengths`: some block-row of some left tile has all 8 slots live. `right_places`: within one right tile the 32 slots name distinct places. `right_count`: some right tile has all 32 slots live.
All inputs are finite; a program needn't handle non-finite values.
Results may differ from the reference program's by a relative error of at most 0.0003.
Values may be sent and summed in bfloat16 or wider, within the bound.
No kernel may reach another device: no remote copies, remote signals or barrier semaphores. Data moves between devices by JAX's collectives and lax.ppermute only.
A program may use at most 192 MiB of HBM per device.

```python
import jax
import jax.numpy as jnp
from jax import lax

BS = 64
BRC = 8
ROW_SLOTS = 8
KB = 16
BCR = 16
CAP_B = 32
N_ROW = 16
N_COL = 2


def draw_left_slots(key, part):
    tile_keys = jax.random.split(key, N_COL * N_COL * BRC)
    chosen = jax.vmap(lambda one_key: jax.random.permutation(one_key, KB)[:ROW_SLOTS])(tile_keys)
    return chosen.reshape(N_COL, N_COL, BRC * ROW_SLOTS).astype(jnp.int32)


def draw_left_lengths(key, part):
    light_key = jax.random.fold_in(key, 11)
    heavy_key = jax.random.fold_in(key, 12)
    pick_key = jax.random.fold_in(key, 13)
    light = jax.random.randint(light_key, (N_COL, N_COL, BRC), 1, ROW_SLOTS // 2 + 1)
    heavy = jax.random.randint(heavy_key, (N_COL, 1, BRC), 0, 4) == 0
    first_row = jax.random.randint(pick_key, (), 0, BRC)
    heavy = heavy.at[0, 0, first_row].set(True)
    heavy = jnp.broadcast_to(heavy, (N_COL, N_COL, BRC))
    return jnp.where(heavy, ROW_SLOTS, light).astype(jnp.int32)


def draw_right_places(key, part):
    tile_keys = jax.random.split(key, N_COL * N_ROW)
    chosen = jax.vmap(lambda one_key: jax.random.permutation(one_key, KB * BCR)[:CAP_B])(tile_keys)
    return chosen.reshape(N_COL, N_ROW, CAP_B).astype(jnp.int32)


def draw_right_count(key, part):
    count_key = jax.random.fold_in(key, 21)
    pick_key = jax.random.fold_in(key, 22)
    counts = jax.random.randint(count_key, (N_COL, N_ROW), 1, CAP_B + 1)
    full_tile = jax.random.randint(pick_key, (), 0, N_ROW)
    counts = counts.at[0, full_tile].set(CAP_B)
    return counts.astype(jnp.int32)


def steps_of(rng, shape, cuts, smallest, top_value):
    loudness, own = 1.0, jax.random.fold_in(rng, 6)
    for axis_at, shards_of in cuts:
        draws = jnp.exp(jax.random.uniform(jax.random.fold_in(own, axis_at), (shards_of,), jnp.float32, smallest / len(cuts), top_value / len(cuts)))
        loudness = loudness * jnp.repeat(draws, shape[axis_at] // shards_of).reshape([-1 if axis == axis_at else 1 for axis in range(len(shape))])
    return loudness


def noise(own_key, shape, deviation, most, cuts=(), kind=jnp.bfloat16):
    array = deviation * jax.random.normal(own_key, shape, jnp.float32)
    if cuts:
        array = array * steps_of(own_key, shape, cuts, -0.22, 0.18)
    return jnp.clip(array, -most, most).astype(kind)


def setup_inputs(seed: int = 0) -> dict:
    key_of = jax.random.split(jax.random.key(seed), 7)
    left_blocks = noise(key_of[0], (N_COL, N_COL, BRC * ROW_SLOTS, BS * BS), BS ** -0.5, 0.75, ((0, 2), (2, 16)))
    left_slots = draw_left_slots(jax.random.fold_in(key_of[6], 71), 0)
    left_lengths = draw_left_lengths(jax.random.fold_in(key_of[6], 71), 0)
    right_blocks = noise(key_of[3], (N_COL, N_ROW, CAP_B, BS * BS), 1.0, 6.0, ((0, 2), (1, 16)))
    right_places = draw_right_places(jax.random.fold_in(key_of[6], 71), 0)
    right_count = draw_right_count(jax.random.fold_in(key_of[6], 71), 0)
    return dict(left_blocks=left_blocks, left_slots=left_slots, left_lengths=left_lengths, right_blocks=right_blocks, right_places=right_places, right_count=right_count)


def densify_right(values, places, live_count):
    slot_index = jnp.arange(values.shape[0], dtype=jnp.int32)
    live_mask = slot_index < live_count
    kept_values = jnp.where(live_mask[:, None], values.astype(jnp.float32), jnp.float32(0))
    dense_tile = jnp.zeros((KB * BCR, BS * BS), jnp.float32).at[places].add(kept_values)
    return dense_tile.reshape(KB, BCR, BS, BS)


def left_tile(values, slots, lengths):
    position = jnp.arange(ROW_SLOTS, dtype=jnp.int32)
    live_mask = (position[None, :] < lengths[:, None]).reshape(-1)
    blocks = jnp.where(live_mask[:, None], values.astype(jnp.float32), jnp.float32(0))
    return blocks.reshape(BRC, ROW_SLOTS, BS, BS), slots.reshape(BRC, ROW_SLOTS)


def tile_product(blocks, columns, dense_tile):
    panels = jnp.take(dense_tile, columns, axis=0)
    return jnp.einsum("ipxa,ipjab->ixjb", blocks, panels, precision=lax.Precision.HIGHEST)


def reference(left_blocks, left_slots, left_lengths, right_blocks, right_places, right_count):
    def one_column(col_group):
        def one_group(running, inner_group):
            dense_tile = densify_right(right_blocks[inner_group, col_group], right_places[inner_group, col_group], right_count[inner_group, col_group])

            def one_row_group(row_group):
                blocks, columns = left_tile(left_blocks[row_group, inner_group], left_slots[row_group, inner_group], left_lengths[row_group, inner_group])
                return tile_product(blocks, columns, dense_tile)

            return running + lax.map(one_row_group, jnp.arange(N_COL, dtype=jnp.int32)), None

        start = jnp.zeros((N_COL, BRC, BS, BCR, BS), jnp.float32)
        running, _ = lax.scan(one_group, start, jnp.arange(N_COL, dtype=jnp.int32))
        return running

    tiles = lax.map(one_column, jnp.arange(N_ROW, dtype=jnp.int32))
    return tiles.transpose(1, 2, 3, 0, 4, 5).reshape(N_COL * BRC * BS, N_ROW * BCR * BS)
```

```python
import functools
import math

import jax
import jax.numpy as jnp
from jax import lax
from jax.experimental import pallas as pl
from jax.experimental.pallas import tpu as pltpu
from jax.sharding import PartitionSpec as P

KB = 16
BCR = 16
LANES = 128
META = 16


def swapped(x, mask):
    peers = lax.axis_size("row")
    return lax.ppermute(x, "row", [(i, i ^ mask) for i in range(peers)])


def low_half(rows):
    return lax.broadcasted_iota(jnp.int32, (rows, LANES), 1) < LANES // 2


def pack_kernel(where_ref, slots_ref, lengths_ref, left_ref, out_ref, tall, square):
    tiles, own, _ = left_ref.shape
    block_rows = lengths_ref.shape[1]
    per_row = where_ref[1]
    first = where_ref[0] * own
    row = lax.div(first, per_row)
    place = lax.rem(first, per_row)
    low = low_half(32)
    low_meta = low_half(META)
    meta_row = lax.broadcasted_iota(jnp.int32, (META, LANES), 0)
    meta = jnp.full((META, LANES), -1.0, jnp.float32)
    at = 0
    for m in range(tiles):
        values = left_ref[m].astype(jnp.float32)
        for t in range(32):
            tall[pl.ds(t * 8, own), :] = values[:, t * LANES : (t + 1) * LANES]
        live = lengths_ref[m, row]
        for s in range(0, own, 2):
            one = tall[pl.ds(s, 32, stride=8), :]
            two = tall[pl.ds(s + 1, 32, stride=8), :]
            even = jnp.where(low, one, pltpu.roll(two, LANES // 2, 1))
            odd = jnp.where(low, pltpu.roll(one, LANES // 2, 1), two)
            square[pl.ds(0, 32, stride=2), :] = even
            square[pl.ds(1, 32, stride=2), :] = odd
            out_ref[at * 64 : at * 64 + 64, :] = square[...].astype(out_ref.dtype)
            a = jnp.where(place + s < live, slots_ref[m, s], -1).astype(jnp.float32)
            b = jnp.where(place + s + 1 < live, slots_ref[m, s + 1], -1).astype(jnp.float32)
            meta = jnp.where(meta_row == at, jnp.where(low_meta, a, b), meta)
            at += 1
    out_ref[at * 64 : at * 64 + META, :] = meta.astype(out_ref.dtype)


def pack(left, slots, lengths, per_row):
    tiles, own, _ = left.shape
    where = jnp.stack([lax.axis_index("row").astype(jnp.int32), jnp.int32(per_row)])
    rows = tiles * own // 2 * 64 + META
    return pl.pallas_call(
        pack_kernel,
        out_shape=jax.ShapeDtypeStruct((rows, LANES), left.dtype),
        in_specs=[pl.BlockSpec(memory_space=pltpu.SMEM)] * 3 + [pl.BlockSpec(memory_space=pltpu.VMEM)],
        out_specs=pl.BlockSpec(memory_space=pltpu.VMEM),
        scratch_shapes=[pltpu.VMEM((256, LANES), jnp.float32), pltpu.VMEM((64, LANES), jnp.float32)],
    )(where, slots, lengths, left)


def repeat(count, body):
    if count <= 2:
        for i in range(count):
            body(i)
    else:
        pl.loop(0, count)(body)


def place_right(values_ref, places_ref, count_ref, dense_ref, base, tall, square):
    slots = values_ref.shape[0]
    half = lax.broadcasted_iota(jnp.int32, (32, LANES), 1) // (LANES // 2)
    count = count_ref[0, 0]

    def some(g):
        values = values_ref[pl.ds(g * 16, 16), :].astype(jnp.float32)
        for t in range(32):
            tall[pl.ds(t * 16, 16), :] = values[:, t * LANES : (t + 1) * LANES]
        for s in range(16):
            spot = places_ref[0, g * 16 + s]
            live = g * 16 + s < count
            k, j = lax.shift_right_logical(spot, 4), lax.bitwise_and(spot, 15)
            side = lax.bitwise_and(j, 1)
            plain = tall[pl.ds(s, 32, stride=16), :]
            turned = pltpu.roll(plain, LANES // 2, 1)
            keep = half == jnp.where(live, side, -1)
            even = jnp.where(keep, jnp.where(side == 0, plain, turned), 0.0)
            odd = jnp.where(keep, jnp.where(side == 0, turned, plain), 0.0)
            y = square.at[s % square.shape[0]]
            y[pl.ds(0, 32, stride=2), :] = even
            y[pl.ds(1, 32, stride=2), :] = odd
            at = (
                pl.ds(pl.multiple_of(base + k * 64, 64), 64),
                pl.ds(pl.multiple_of(lax.shift_right_logical(j, 1) * LANES, LANES), LANES),
            )
            dense_ref[at] = dense_ref[at] + y[...].astype(dense_ref.dtype)

    repeat(slots // 16, some)


def place_left(parcels, row, tiles, pairs, dense_ref, names_ref):
    half = (lax.broadcasted_iota(jnp.int32, (16, LANES), 1) // (LANES // 2)).astype(jnp.float32)
    body = tiles * pairs * 64
    for i, parcel in enumerate(parcels):
        names_ref[i * META : i * META + META, :] = parcel[body : body + META, :].astype(jnp.float32)

    def one(m):
        names = []
        for i, parcel in enumerate(parcels):
            for p in range(pairs):
                at = m * pairs + p
                name = jnp.broadcast_to(names_ref[pl.ds(i * META + at, 1), :], (16, LANES))
                turned = pltpu.roll(name, LANES // 2, 1)
                names.append((parcel, at * 64, (name - half).astype(jnp.bfloat16), (turned - half).astype(jnp.bfloat16)))
        for c in range(4):
            blocks = []
            for parcel, start, a, b in names:
                v = parcel[pl.ds(start + c * 16, 16), :]
                w = pltpu.roll(v.astype(jnp.float32), LANES // 2, 1).astype(v.dtype)
                blocks.append((v, w, a, b))
            for t in range(KB // 2):
                want = jnp.bfloat16(2 * t)
                acc = jnp.zeros((16, LANES), dense_ref.dtype)
                for v, w, a, b in blocks:
                    acc = jnp.where(a == want, v, acc)
                    acc = jnp.where(b == want, w, acc)
                dense_ref[
                    pl.ds(pl.multiple_of(row * 64 + c * 16, 16), 16),
                    pl.ds(pl.multiple_of(m * KB * 64 + t * LANES, LANES), LANES),
                ] = acc

    repeat(tiles, one)


def product_kernel(tiles, pairs, masks, per_row, *refs):
    where_ref = refs[0]
    refs = refs[1:]
    places, refs = refs[:tiles], refs[tiles:]
    counts, refs = refs[:tiles], refs[tiles:]
    rights, refs = refs[:tiles], refs[tiles:]
    parcels, refs = dict(zip(masks, refs[: len(masks)])), refs[len(masks) :]
    out_ref, left_dense, right_dense, result, tall, square, names, sems = refs
    me = where_ref[0]
    first = where_ref[1]
    right_dense[...] = jnp.zeros_like(right_dense)
    for m in range(tiles):
        group = lax.rem(first - m + tiles, tiles)
        place_right(rights[m], places[m], counts[m], right_dense, group * KB * 64, tall, square)
    sharing = per_row // (2 * pairs)
    for base in range(0, len(masks), sharing):
        row = lax.div(lax.bitwise_xor(me, base), sharing)
        place_left([parcels[base + i] for i in range(sharing)], row, tiles, pairs, left_dense, names)
    width = 256
    copies = []
    for n in range(out_ref.shape[1] // width):
        span = slice(n * width, n * width + width)
        if tiles <= 2:
            result[:, span] = jnp.dot(left_dense[...], right_dense[:, span], preferred_element_type=jnp.float32)
        else:
            result[:, span] = jnp.zeros_like(result[:, span])

            @pl.loop(0, tiles)
            def _(m, span=span):
                part = pl.ds(pl.multiple_of(m * KB * 64, KB * 64), KB * 64)
                result[:, span] += jnp.dot(left_dense[:, part], right_dense[part, span], preferred_element_type=jnp.float32)

        copy = pltpu.make_async_copy(result.at[:, span], out_ref.at[:, span], sems.at[n])
        copy.start()
        copies.append(copy)
    for copy in copies:
        copy.wait()


def shards(left_blocks, left_slots, left_lengths, right_blocks, right_places, right_count):
    peers = lax.axis_size("row")
    cols = lax.axis_size("col")
    tiles, own = left_blocks.shape[1], left_blocks.shape[2]
    block_rows = left_lengths.shape[2]
    per_row = peers * own // block_rows
    pairs = own // 2
    side = math.isqrt(left_blocks.shape[-1])

    def from_col(x, by):
        return x if by == 0 else lax.ppermute(x, "col", [(i, (i + by) % cols) for i in range(cols)])

    rights, places, counts = [], [], []
    for by in range(cols):
        places.append(from_col(right_places[0], by))
        counts.append(from_col(right_count, by))
        rights.append(from_col(right_blocks[0, 0], by))
    parcel = pack(left_blocks[0], left_slots[0], left_lengths[0], per_row)
    held = {0: parcel}
    for mask in range(4, peers, 4):
        held[mask] = swapped(parcel, mask)
    for mask in range(0, peers, 4):
        held[mask + 2] = swapped(held[mask], 2)
    for mask in range(0, peers, 2):
        held[mask + 1] = swapped(held[mask], 1)
    masks = list(range(peers))
    where = jnp.stack([lax.axis_index("row").astype(jnp.int32), lax.axis_index("col").astype(jnp.int32)])
    height, depth, width = block_rows * side, tiles * KB * side, BCR * side
    smem, vmem = pl.BlockSpec(memory_space=pltpu.SMEM), pl.BlockSpec(memory_space=pltpu.VMEM)
    return pl.pallas_call(
        functools.partial(product_kernel, tiles, pairs, masks, per_row),
        out_shape=jax.ShapeDtypeStruct((height, width), jnp.float32),
        in_specs=[smem] * (1 + 2 * tiles) + [vmem] * (tiles + peers),
        out_specs=pl.BlockSpec(memory_space=pltpu.HBM),
        scratch_shapes=[
            pltpu.VMEM((height, depth), left_blocks.dtype),
            pltpu.VMEM((depth, width), left_blocks.dtype),
            pltpu.VMEM((height, width), jnp.float32),
            pltpu.VMEM((512, LANES), jnp.float32),
            pltpu.VMEM((4, side, LANES), jnp.float32),
            pltpu.VMEM((per_row // own * META, LANES), jnp.float32),
            pltpu.SemaphoreType.DMA((width // 256,)),
        ],
        compiler_params=pltpu.CompilerParams(vmem_limit_bytes=40 * 1024 * 1024),
    )(where, *places, *counts, *rights, *[held[m] for m in masks])


def solution(mesh):
    return jax.shard_map(
        shards,
        mesh=mesh,
        in_specs=(
            P("col", None, "row", None),
            P("col", None, "row"),
            P("col", None, None),
            P("col", "row", None, None),
            P("col", "row", None),
            P("col", "row"),
        ),
        out_specs=P("col", "row"),
        check_vma=False,
    )
```

```python
import functools
import math

import jax
import jax.numpy as jnp
from jax import lax
from jax.experimental import pallas as pl
from jax.experimental.pallas import tpu as pltpu
from jax.sharding import PartitionSpec as P

KB = 16
BCR = 16
LANES = 128
META = 16


def swapped(x, mask):
    peers = lax.axis_size("row")
    return lax.ppermute(x, "row", [(i, i ^ mask) for i in range(peers)])


def low_half(rows):
    return lax.broadcasted_iota(jnp.int32, (rows, LANES), 1) < LANES // 2


def pick_lane(row, at):
    lane = lax.broadcasted_iota(jnp.int32, row.shape, 1)
    return jnp.sum(jnp.where(lane == at, row, 0.0), axis=1, keepdims=True)


def pack_kernel(start, masks, slots_ref, lengths_ref, left_ref, *refs):
    out_ref, tall, square = refs[-3:]
    tiles, own, _ = left_ref.shape
    peers = lax.axis_size("row")
    me = lax.axis_index("row")
    mask = masks[0] if masks[0] == masks[1] else jnp.where(lax.rem(me, 2) == 0, masks[0], masks[1])
    per_row = peers * own // lengths_ref.shape[1]
    first = lax.bitwise_xor(me, mask) * own
    row = lax.div(first, per_row)
    place = lax.rem(first, per_row)
    group = lax.axis_index("col")
    low = low_half(32)
    low_meta = low_half(META)
    meta_row = lax.broadcasted_iota(jnp.int32, (META, LANES), 0)
    meta = jnp.full((META, LANES), -1.0, jnp.float32)
    at = 0
    for by in range(tiles):
        m = lax.rem(group - by + tiles, tiles)
        values = left_ref[m].astype(jnp.float32)
        for t in range(32):
            tall[pl.ds(by % 2 * 256 + t * 8, own), :] = values[:, t * LANES : (t + 1) * LANES]
        named = slots_ref[pl.ds(m, 1), :].astype(jnp.float32)
        live = pick_lane(lengths_ref[pl.ds(m, 1), :].astype(jnp.float32), row)
        for s in range(0, own, 2):
            one = tall[pl.ds(by % 2 * 256 + s, 32, stride=8), :]
            two = tall[pl.ds(by % 2 * 256 + s + 1, 32, stride=8), :]
            even = jnp.where(low, one, pltpu.roll(two, LANES // 2, 1))
            odd = jnp.where(low, pltpu.roll(one, LANES // 2, 1), two)
            y = square.at[at % 4]
            y[pl.ds(0, 32, stride=2), :] = even
            y[pl.ds(1, 32, stride=2), :] = odd
            out_ref[start + at * 64 : start + at * 64 + 64, :] = y[...].astype(out_ref.dtype)
            a = jnp.where((place + s).astype(jnp.float32) < live, pick_lane(named, s), -1.0)
            b = jnp.where((place + s + 1).astype(jnp.float32) < live, pick_lane(named, s + 1), -1.0)
            meta = jnp.where(meta_row == at, jnp.where(low_meta, a, b), meta)
            at += 1
    out_ref[start + at * 64 : start + at * 64 + META, :] = meta.astype(out_ref.dtype)


def pack(left, slots, lengths, masks=(0, 0), parts=1, part=0, buffer=None):
    tiles, own, _ = left.shape
    rows = tiles * own // 2 * 64 + META
    vmem = pl.BlockSpec(memory_space=pltpu.VMEM)
    given = [] if buffer is None else [buffer]
    return pl.pallas_call(
        functools.partial(pack_kernel, part * rows, masks),
        out_shape=jax.ShapeDtypeStruct((parts * rows, LANES), left.dtype),
        in_specs=[vmem] * (3 + len(given)),
        out_specs=vmem,
        scratch_shapes=[pltpu.VMEM((512, LANES), jnp.float32), pltpu.VMEM((4, 64, LANES), jnp.float32)],
        input_output_aliases={3: 0} if given else {},
        compiler_params=pltpu.CompilerParams(vmem_limit_bytes=4 * 1024 * 1024),
        cost_estimate=pl.CostEstimate(flops=1000000, bytes_accessed=1000, transcendentals=0),
    )(slots, lengths, left, *given)


def spots_kernel(count_ref, places_ref, out_ref):
    slot = lax.broadcasted_iota(jnp.int32, places_ref.shape, 1)
    out_ref[...] = jnp.where(slot < count_ref[0, 0], places_ref[...], -1)


def live_spots(places, count):
    smem, vmem = pl.BlockSpec(memory_space=pltpu.SMEM), pl.BlockSpec(memory_space=pltpu.VMEM)
    return pl.pallas_call(
        spots_kernel,
        out_shape=jax.ShapeDtypeStruct(places.shape, places.dtype),
        in_specs=[smem, vmem],
        out_specs=vmem,
        compiler_params=pltpu.CompilerParams(vmem_limit_bytes=1024 * 1024),
    )(count, places)


def repeat(count, body):
    if count <= 2:
        for i in range(count):
            body(i)
    else:
        pl.loop(0, count)(body)


def right_kernel(places_ref, values_ref, dense_ref, tall, square):
    slots = values_ref.shape[0]
    half = lax.broadcasted_iota(jnp.int32, (32, LANES), 1) // (LANES // 2)
    dense_ref[...] = jnp.zeros_like(dense_ref)

    def some(g):
        values = values_ref[pl.ds(g * 16, 16), :].astype(jnp.float32)
        for t in range(32):
            tall[pl.ds(t * 16, 16), :] = values[:, t * LANES : (t + 1) * LANES]
        for s in range(16):
            spot = places_ref[0, g * 16 + s]
            live = spot >= 0
            spot = jnp.maximum(spot, 0)
            k, j = lax.shift_right_logical(spot, 4), lax.bitwise_and(spot, 15)
            side = lax.bitwise_and(j, 1)
            plain = tall[pl.ds(s, 32, stride=16), :]
            turned = pltpu.roll(plain, LANES // 2, 1)
            keep = half == jnp.where(live, side, -1)
            even = jnp.where(keep, jnp.where(side == 0, plain, turned), 0.0)
            odd = jnp.where(keep, jnp.where(side == 0, turned, plain), 0.0)
            y = square.at[s % square.shape[0]]
            y[pl.ds(0, 32, stride=2), :] = even
            y[pl.ds(1, 32, stride=2), :] = odd
            at = (
                pl.ds(pl.multiple_of(k * 64, 64), 64),
                pl.ds(pl.multiple_of(lax.shift_right_logical(j, 1) * LANES, LANES), LANES),
            )
            dense_ref[at] = dense_ref[at] + y[...].astype(dense_ref.dtype)

    repeat(slots // 16, some)


def dense_right(values, spots):
    side = math.isqrt(values.shape[1])
    smem, vmem = pl.BlockSpec(memory_space=pltpu.SMEM), pl.BlockSpec(memory_space=pltpu.VMEM)
    return pl.pallas_call(
        right_kernel,
        out_shape=jax.ShapeDtypeStruct((KB * side, BCR * side), values.dtype),
        in_specs=[smem, vmem],
        out_specs=vmem,
        scratch_shapes=[pltpu.VMEM((512, LANES), jnp.float32), pltpu.VMEM((4, side, LANES), jnp.float32)],
        compiler_params=pltpu.CompilerParams(vmem_limit_bytes=16 * 1024 * 1024),
        cost_estimate=pl.CostEstimate(flops=1300000000, bytes_accessed=1000, transcendentals=0),
    )(spots, values)


def place_left(parcels, row, tiles, pairs, dense_ref, names_ref):
    half = (lax.broadcasted_iota(jnp.int32, (16, LANES), 1) // (LANES // 2)).astype(jnp.float32)
    body = tiles * pairs * 64
    for i, (parcel, start) in enumerate(parcels):
        names_ref[i * META : i * META + META, :] = parcel[pl.ds(start + body, META), :].astype(jnp.float32)

    def one(m):
        names = []
        for i, (parcel, start) in enumerate(parcels):
            for p in range(pairs):
                at = m * pairs + p
                name = jnp.broadcast_to(names_ref[pl.ds(i * META + at, 1), :], (16, LANES))
                turned = pltpu.roll(name, LANES // 2, 1)
                names.append((parcel, start + at * 64, (name - half).astype(jnp.bfloat16), (turned - half).astype(jnp.bfloat16)))
        plain, turned = [], []
        for parcel, start, _, _ in names:
            v = [parcel[pl.ds(start + c * 16, 16), :] for c in range(4)]
            plain.append(v)
            turned.append([pltpu.roll(x.astype(jnp.float32), LANES // 2, 1).astype(x.dtype) for x in v])
        for t in range(KB // 2):
            want = jnp.bfloat16(2 * t)
            hits = [(a == want, b == want) for _, _, a, b in names]
            for c in range(4):
                acc = jnp.zeros((16, LANES), dense_ref.dtype)
                for (a, b), v, w in zip(hits, plain, turned):
                    acc = jnp.where(a, v[c], acc)
                    acc = jnp.where(b, w[c], acc)
                dense_ref[
                    pl.ds(row * 64 + c * 16, 16),
                    pl.ds(pl.multiple_of(m * KB * 64 + t * LANES, LANES), LANES),
                ] = acc

    repeat(tiles, one)


def product_kernel(tiles, pairs, jobs, stacks, first_call, *refs):
    rights, refs = refs[:tiles], refs[tiles:]
    held, refs = refs[:stacks], refs[stacks:]
    if not first_call:
        refs = refs[1:]
    out_ref, left_dense, result, names, sems = refs
    sharing = names.shape[0] // META
    size = tiles * pairs * 64 + META
    me = lax.axis_index("row")
    core = lax.rem(me, 2)

    def pick(pair):
        return pair[0] if pair[0] == pair[1] else jnp.where(core == 0, pair[0], pair[1])

    for i, (_, parts) in enumerate(jobs):
        parcels = []
        for at, zero, one in parts:
            start = pick((zero * size, one * size))
            parcels.append((held[at], start if isinstance(start, int) else pl.multiple_of(start, 16)))
        place_left(parcels, i, tiles, pairs, left_dense, names)
    width = 256
    depth = rights[0].shape[0]
    copies = []
    for n in range(out_ref.shape[1] // width):
        span = slice(n * width, n * width + width)
        total = None
        for m in range(tiles):
            part = jnp.dot(
                left_dense[:, m * depth : m * depth + depth],
                rights[m][:, span],
                preferred_element_type=jnp.float32,
            )
            total = part if total is None else total + part
        result[:, span] = total
        if n % 2 == 1:
            wide = slice(n * width - width, n * width + width)
            for i, (masks, _) in enumerate(jobs):
                row = lax.div(lax.bitwise_xor(me, pick(masks)), sharing)
                copies.append(
                    pltpu.make_async_copy(
                        result.at[pl.ds(i * 64, 64), wide],
                        out_ref.at[pl.ds(pl.multiple_of(row * 64, 64), 64), wide],
                        sems.at[n // 2, i],
                    )
                )
                copies[-1].start()
    for copy in copies:
        copy.wait()


def product(rights, stacks, jobs, sharing, height, pairs, before=None):
    depth, width = rights[0].shape
    tiles, dtype = len(rights), rights[0].dtype
    rows = len(jobs) * 64
    vmem, hbm = pl.BlockSpec(memory_space=pltpu.VMEM), pl.BlockSpec(memory_space=pltpu.HBM)
    first = before is None
    return pl.pallas_call(
        functools.partial(product_kernel, tiles, pairs, jobs, len(stacks), first),
        out_shape=jax.ShapeDtypeStruct((height, width), jnp.float32),
        in_specs=[vmem] * (tiles + len(stacks)) + ([] if first else [hbm]),
        out_specs=hbm,
        scratch_shapes=[
            pltpu.VMEM((rows, tiles * depth), dtype),
            pltpu.VMEM((rows, width), jnp.float32),
            pltpu.VMEM((sharing * META, LANES), jnp.float32),
            pltpu.SemaphoreType.DMA((width // 512, len(jobs))),
        ],
        input_output_aliases={} if first else {tiles + len(stacks): 0},
        compiler_params=pltpu.CompilerParams(vmem_limit_bytes=(8 + 5 * tiles) * 1024 * 1024),
        cost_estimate=pl.CostEstimate(
            flops=2000000000, bytes_accessed=1000, transcendentals=0
        ),
    )(*rights, *stacks, *([] if first else [before]))


def fill_kernel(start, part_ref, *refs):
    refs[-1][start : start + part_ref.shape[0], :] = part_ref[...]


def fill(part, rows, start=0, buffer=None):
    vmem = pl.BlockSpec(memory_space=pltpu.VMEM)
    given = [] if buffer is None else [buffer]
    return pl.pallas_call(
        functools.partial(fill_kernel, start),
        out_shape=jax.ShapeDtypeStruct((rows, LANES), part.dtype),
        in_specs=[vmem] * (1 + len(given)),
        out_specs=vmem,
        input_output_aliases={1: 0} if given else {},
        compiler_params=pltpu.CompilerParams(vmem_limit_bytes=4 * 1024 * 1024),
        cost_estimate=pl.CostEstimate(flops=1000000, bytes_accessed=1000, transcendentals=0),
    )(part, *given)


def by_core(x, zero, one):
    peers = lax.axis_size("row")
    return lax.ppermute(x, "row", [(i, i ^ (one if i % 2 else zero)) for i in range(peers)])


def spread(order):
    names = [0]
    for mask in order:
        names = names + [name ^ mask for name in names]
    return names


def shards(left_blocks, left_slots, left_lengths, right_blocks, right_places, right_count):
    peers = lax.axis_size("row")
    cols = lax.axis_size("col")
    tiles, own = left_blocks.shape[1], left_blocks.shape[2]
    block_rows = left_lengths.shape[2]
    sharing = peers // block_rows
    side = math.isqrt(left_blocks.shape[-1])
    height = block_rows * side

    def from_col(x, by):
        return x if by == 0 else lax.ppermute(x, "col", [(i, (i + by) % cols) for i in range(cols)])

    left, slots, lengths = left_blocks[0], left_slots[0], left_lengths[0]
    own_right = right_blocks[0, 0]

    if sharing == 2:
        bits = [1 << b for b in range(1, peers.bit_length() - 1)]
        zero = bits[-1:] + bits[:-1]
        one = bits[-1:] + bits[1:-1] + bits[:1]
        first = (zero[0], one[0])
        come = by_core(left, *first), by_core(slots, *first)
        stack = pack(left, slots, lengths, parts=2)
        sending, stack = lax.optimization_barrier((own_right, stack))
        stack = pack(come[0], come[1], lengths, first, parts=2, part=1, buffer=stack)
        rights = []
        for step, (a, b) in enumerate(zip(zero[1:-1], one[1:-1])):
            new = by_core(stack, a, b)
            rows = stack.shape[0]
            wide = fill(stack, 2 * rows)
            if step == 0:
                wide, places, count = lax.optimization_barrier((wide, right_places[0], right_count))
                spots = live_spots(places, count)
                sent = [from_col(sending, by) for by in range(1, cols)]
                places = [from_col(spots, by) for by in range(1, cols)]
            stack = fill(new, 2 * rows, rows, wide)
        late, stack = lax.optimization_barrier((spots, stack))
        rights = [dense_right(own_right, late)]
        rights += [dense_right(x, p) for x, p in zip(sent, places)]
        last = by_core(stack, zero[-1], one[-1])
        held = [[stack, last], [swapped(stack, 1), None]]
        at_zero, at_one = spread(zero), spread(one)
        count = len(at_zero) // 2
        kinds = {}
        for name in at_zero:
            p, q = at_zero.index(name), at_one.index(name)
            kinds.setdefault((p // count, q // count), []).append((name, p % count, q % count))

        def jobs(mine, theirs):
            zeros, ones = kinds.get((mine, theirs), []), kinds.get((theirs, mine), [])
            return [
                ((a, b), (mine, a_own, b_own), (theirs, a_other, b_other))
                for (a, a_own, a_other), (b, b_other, b_own) in zip(zeros, ones)
            ]

        out = None
        for group in ([(0, 0)], [(1, 0)], [(0, 1), (1, 1)]):
            arrays, keys, listed = [], {}, []

            def key(whose, part):
                if (whose, part) not in keys:
                    keys[whose, part] = len(arrays)
                    arrays.append(held[whose][part])
                return keys[whose, part]

            for mine, theirs in group:
                for masks, (m, x, y), (t, u, v) in jobs(mine, theirs):
                    listed.append((masks, [(key(0, m), x, y), (key(1, t), u, v)]))
            if listed:
                out = product(rights, arrays, listed, sharing, height, own // 2, out)
            if held[1][1] is None:
                held[0][1], out = lax.optimization_barrier((held[0][1], out))
                held[1][1] = swapped(held[0][1], 1)
        return out
    spots = live_spots(right_places[0], right_count)
    rights = [dense_right(from_col(own_right, by), from_col(spots, by)) for by in range(cols)]
    parcel = pack(left, slots, lengths)
    held = {0: parcel}
    for mask in range(4, peers, 4):
        held[mask] = swapped(parcel, mask)
    for mask in range(0, peers, 4):
        held[mask + 2] = swapped(held[mask], 2)
    for mask in range(0, peers, 2):
        held[mask + 1] = swapped(held[mask], 1)
    half = None
    for names in (range(peers // 2), range(peers // 2, peers)):
        listed = [
            ((names[i], names[i]), [(i + j, 0, 0) for j in range(sharing)]) for i in range(0, len(names), sharing)
        ]
        half = product(rights, [held[n] for n in names], listed, sharing, height, own // 2, half)
    return half


def solution(mesh):
    return jax.shard_map(
        shards,
        mesh=mesh,
        in_specs=(
            P("col", None, "row", None),
            P("col", None, "row"),
            P("col", None, None),
            P("col", "row", None, None),
            P("col", "row", None),
            P("col", "row"),
        ),
        out_specs=P("col", "row"),
        check_vma=False,
    )
```

```python
import functools
import math

import jax
import jax.numpy as jnp
from jax import lax
from jax.experimental import pallas as pl
from jax.experimental.pallas import tpu as pltpu
from jax.sharding import PartitionSpec as P

KB = 16
BCR = 16
LANES = 128
META = 16


def swapped(x, mask):
    peers = lax.axis_size("row")
    return lax.ppermute(x, "row", [(i, i ^ mask) for i in range(peers)])


def low_half(rows):
    return lax.broadcasted_iota(jnp.int32, (rows, LANES), 1) < LANES // 2


def pick_lane(row, at):
    lane = lax.broadcasted_iota(jnp.int32, row.shape, 1)
    return jnp.sum(jnp.where(lane == at, row, 0.0), axis=1, keepdims=True)


def pack_kernel(start, masks, slots_ref, lengths_ref, left_ref, *refs):
    out_ref, tall, square = refs[-3:]
    tiles, own, _ = left_ref.shape
    peers = lax.axis_size("row")
    me = lax.axis_index("row")
    mask = masks[0] if masks[0] == masks[1] else jnp.where(lax.rem(me, 2) == 0, masks[0], masks[1])
    per_row = peers * own // lengths_ref.shape[1]
    first = lax.bitwise_xor(me, mask) * own
    row = lax.div(first, per_row)
    place = lax.rem(first, per_row)
    group = lax.axis_index("col")
    low = low_half(32)
    low_meta = low_half(META)
    meta_row = lax.broadcasted_iota(jnp.int32, (META, LANES), 0)
    meta = jnp.full((META, LANES), -1.0, jnp.float32)
    at = 0
    for by in range(tiles):
        m = lax.rem(group - by + tiles, tiles)
        values = left_ref[m].astype(jnp.float32)
        for t in range(32):
            tall[pl.ds(by % 2 * 256 + t * 8, own), :] = values[:, t * LANES : (t + 1) * LANES]
        named = slots_ref[pl.ds(m, 1), :].astype(jnp.float32)
        live = pick_lane(lengths_ref[pl.ds(m, 1), :].astype(jnp.float32), row)
        for s in range(0, own, 2):
            one = tall[pl.ds(by % 2 * 256 + s, 32, stride=8), :]
            two = tall[pl.ds(by % 2 * 256 + s + 1, 32, stride=8), :]
            even = jnp.where(low, one, pltpu.roll(two, LANES // 2, 1))
            odd = jnp.where(low, pltpu.roll(one, LANES // 2, 1), two)
            y = square.at[at % 4]
            y[pl.ds(0, 32, stride=2), :] = even
            y[pl.ds(1, 32, stride=2), :] = odd
            out_ref[start + at * 64 : start + at * 64 + 64, :] = y[...].astype(out_ref.dtype)
            a = jnp.where((place + s).astype(jnp.float32) < live, pick_lane(named, s), -1.0)
            b = jnp.where((place + s + 1).astype(jnp.float32) < live, pick_lane(named, s + 1), -1.0)
            meta = jnp.where(meta_row == at, jnp.where(low_meta, a, b), meta)
            at += 1
    out_ref[start + at * 64 : start + at * 64 + META, :] = meta.astype(out_ref.dtype)


def pack(left, slots, lengths, masks=(0, 0), parts=1, part=0, buffer=None):
    tiles, own, _ = left.shape
    rows = tiles * own // 2 * 64 + META
    vmem = pl.BlockSpec(memory_space=pltpu.VMEM)
    given = [] if buffer is None else [buffer]
    return pl.pallas_call(
        functools.partial(pack_kernel, part * rows, masks),
        out_shape=jax.ShapeDtypeStruct((parts * rows, LANES), left.dtype),
        in_specs=[vmem] * (3 + len(given)),
        out_specs=vmem,
        scratch_shapes=[pltpu.VMEM((512, LANES), jnp.float32), pltpu.VMEM((4, 64, LANES), jnp.float32)],
        input_output_aliases={3: 0} if given else {},
        compiler_params=pltpu.CompilerParams(vmem_limit_bytes=4 * 1024 * 1024),
        cost_estimate=pl.CostEstimate(flops=2 * 10**9, bytes_accessed=1000, transcendentals=0),
    )(slots, lengths, left, *given)


def spots_kernel(count_ref, places_ref, out_ref):
    slot = lax.broadcasted_iota(jnp.int32, places_ref.shape, 1)
    out_ref[...] = jnp.where(slot < count_ref[0, 0], places_ref[...], -1)


def live_spots(places, count):
    smem, vmem = pl.BlockSpec(memory_space=pltpu.SMEM), pl.BlockSpec(memory_space=pltpu.VMEM)
    return pl.pallas_call(
        spots_kernel,
        out_shape=jax.ShapeDtypeStruct(places.shape, places.dtype),
        in_specs=[smem, vmem],
        out_specs=vmem,
        compiler_params=pltpu.CompilerParams(vmem_limit_bytes=1024 * 1024),
        cost_estimate=pl.CostEstimate(flops=10**9, bytes_accessed=1000, transcendentals=0),
    )(count, places)


def repeat(count, body):
    if count <= 2:
        for i in range(count):
            body(i)
    else:
        pl.loop(0, count)(body)


def right_kernel(places_ref, values_ref, dense_ref, tall, square):
    slots = values_ref.shape[0]
    half = lax.broadcasted_iota(jnp.int32, (32, LANES), 1) // (LANES // 2)
    dense_ref[...] = jnp.zeros_like(dense_ref)

    def some(g):
        values = values_ref[pl.ds(g * 16, 16), :].astype(jnp.float32)
        for t in range(32):
            tall[pl.ds(t * 16, 16), :] = values[:, t * LANES : (t + 1) * LANES]
        for s in range(16):
            spot = places_ref[0, g * 16 + s]
            live = spot >= 0
            spot = jnp.maximum(spot, 0)
            k, j = lax.shift_right_logical(spot, 4), lax.bitwise_and(spot, 15)
            side = lax.bitwise_and(j, 1)
            plain = tall[pl.ds(s, 32, stride=16), :]
            turned = pltpu.roll(plain, LANES // 2, 1)
            keep = half == jnp.where(live, side, -1)
            even = jnp.where(keep, jnp.where(side == 0, plain, turned), 0.0)
            odd = jnp.where(keep, jnp.where(side == 0, turned, plain), 0.0)
            y = square.at[s % square.shape[0]]
            y[pl.ds(0, 32, stride=2), :] = even
            y[pl.ds(1, 32, stride=2), :] = odd
            at = (
                pl.ds(pl.multiple_of(k * 64, 64), 64),
                pl.ds(pl.multiple_of(lax.shift_right_logical(j, 1) * LANES, LANES), LANES),
            )
            dense_ref[at] = dense_ref[at] + y[...].astype(dense_ref.dtype)

    repeat(slots // 16, some)


def dense_right(values, spots, work=0):
    side = math.isqrt(values.shape[1])
    smem, vmem = pl.BlockSpec(memory_space=pltpu.SMEM), pl.BlockSpec(memory_space=pltpu.VMEM)
    return pl.pallas_call(
        right_kernel,
        out_shape=jax.ShapeDtypeStruct((KB * side, BCR * side), values.dtype),
        in_specs=[smem, vmem],
        out_specs=vmem,
        scratch_shapes=[pltpu.VMEM((512, LANES), jnp.float32), pltpu.VMEM((4, side, LANES), jnp.float32)],
        compiler_params=pltpu.CompilerParams(vmem_limit_bytes=16 * 1024 * 1024),
        cost_estimate=pl.CostEstimate(flops=work, bytes_accessed=1000, transcendentals=0),
    )(spots, values)


def place_left(parcels, row, tiles, pairs, dense_ref, names_ref):
    half = (lax.broadcasted_iota(jnp.int32, (16, LANES), 1) // (LANES // 2)).astype(jnp.float32)
    body = tiles * pairs * 64
    for i, (parcel, start) in enumerate(parcels):
        names_ref[i * META : i * META + META, :] = parcel[pl.ds(start + body, META), :].astype(jnp.float32)

    def one(m):
        names = []
        for i, (parcel, start) in enumerate(parcels):
            for p in range(pairs):
                at = m * pairs + p
                name = jnp.broadcast_to(names_ref[pl.ds(i * META + at, 1), :], (16, LANES))
                turned = pltpu.roll(name, LANES // 2, 1)
                names.append((parcel, start + at * 64, (name - half).astype(jnp.bfloat16), (turned - half).astype(jnp.bfloat16)))
        plain, turned = [], []
        for parcel, start, _, _ in names:
            v = [parcel[pl.ds(start + c * 16, 16), :] for c in range(4)]
            plain.append(v)
            turned.append([pltpu.roll(x.astype(jnp.float32), LANES // 2, 1).astype(x.dtype) for x in v])
        for t in range(KB // 2):
            want = jnp.bfloat16(2 * t)
            hits = [(a == want, b == want) for _, _, a, b in names]
            for c in range(4):
                acc = jnp.zeros((16, LANES), dense_ref.dtype)
                for (a, b), v, w in zip(hits, plain, turned):
                    acc = jnp.where(a, v[c], acc)
                    acc = jnp.where(b, w[c], acc)
                dense_ref[
                    pl.ds(row * 64 + c * 16, 16),
                    pl.ds(pl.multiple_of(m * KB * 64 + t * LANES, LANES), LANES),
                ] = acc

    repeat(tiles, one)


def product_kernel(tiles, pairs, jobs, stacks, first_call, *refs):
    rights, refs = refs[:tiles], refs[tiles:]
    held, refs = refs[:stacks], refs[stacks:]
    if not first_call:
        refs = refs[1:]
    out_ref, left_dense, result, names, sems = refs
    sharing = names.shape[0] // META
    size = tiles * pairs * 64 + META
    me = lax.axis_index("row")
    core = lax.rem(me, 2)

    def pick(pair):
        return pair[0] if pair[0] == pair[1] else jnp.where(core == 0, pair[0], pair[1])

    for i, (_, parts) in enumerate(jobs):
        parcels = []
        for at, zero, one in parts:
            start = pick((zero * size, one * size))
            parcels.append((held[at], start if isinstance(start, int) else pl.multiple_of(start, 16)))
        place_left(parcels, i, tiles, pairs, left_dense, names)
    width = 256
    depth = rights[0].shape[0]
    copies = []
    for n in range(out_ref.shape[1] // width):
        span = slice(n * width, n * width + width)
        total = None
        for m in range(tiles):
            part = jnp.dot(
                left_dense[:, m * depth : m * depth + depth],
                rights[m][:, span],
                preferred_element_type=jnp.float32,
            )
            total = part if total is None else total + part
        result[:, span] = total
        if n % 2 == 1:
            wide = slice(n * width - width, n * width + width)
            for i, (masks, _) in enumerate(jobs):
                row = lax.div(lax.bitwise_xor(me, pick(masks)), sharing)
                copies.append(
                    pltpu.make_async_copy(
                        result.at[pl.ds(i * 64, 64), wide],
                        out_ref.at[pl.ds(pl.multiple_of(row * 64, 64), 64), wide],
                        sems.at[n // 2, i],
                    )
                )
                copies[-1].start()
    for copy in copies:
        copy.wait()


def product(rights, stacks, jobs, sharing, height, pairs, before=None):
    depth, width = rights[0].shape
    tiles, dtype = len(rights), rights[0].dtype
    rows = len(jobs) * 64
    vmem, hbm = pl.BlockSpec(memory_space=pltpu.VMEM), pl.BlockSpec(memory_space=pltpu.HBM)
    first = before is None
    return pl.pallas_call(
        functools.partial(product_kernel, tiles, pairs, jobs, len(stacks), first),
        out_shape=jax.ShapeDtypeStruct((height, width), jnp.float32),
        in_specs=[vmem] * (tiles + len(stacks)) + ([] if first else [hbm]),
        out_specs=hbm,
        scratch_shapes=[
            pltpu.VMEM((rows, tiles * depth), dtype),
            pltpu.VMEM((rows, width), jnp.float32),
            pltpu.VMEM((sharing * META, LANES), jnp.float32),
            pltpu.SemaphoreType.DMA((width // 512, len(jobs))),
        ],
        input_output_aliases={} if first else {tiles + len(stacks): 0},
        compiler_params=pltpu.CompilerParams(vmem_limit_bytes=(8 + 5 * tiles) * 1024 * 1024),
        cost_estimate=pl.CostEstimate(
            flops=10**6, bytes_accessed=1000, transcendentals=0
        ),
    )(*rights, *stacks, *([] if first else [before]))


def fill_kernel(start, part_ref, *refs):
    refs[-1][start : start + part_ref.shape[0], :] = part_ref[...]


def fill(part, rows, start=0, buffer=None):
    vmem = pl.BlockSpec(memory_space=pltpu.VMEM)
    given = [] if buffer is None else [buffer]
    return pl.pallas_call(
        functools.partial(fill_kernel, start),
        out_shape=jax.ShapeDtypeStruct((rows, LANES), part.dtype),
        in_specs=[vmem] * (1 + len(given)),
        out_specs=vmem,
        input_output_aliases={1: 0} if given else {},
        compiler_params=pltpu.CompilerParams(vmem_limit_bytes=4 * 1024 * 1024),
        cost_estimate=pl.CostEstimate(flops=1000000, bytes_accessed=1000, transcendentals=0),
    )(part, *given)


def by_core(x, zero, one):
    peers = lax.axis_size("row")
    return lax.ppermute(x, "row", [(i, i ^ (one if i % 2 else zero)) for i in range(peers)])


def spread(order):
    names = [0]
    for mask in order:
        names = names + [name ^ mask for name in names]
    return names


def shards(left_blocks, left_slots, left_lengths, right_blocks, right_places, right_count):
    peers = lax.axis_size("row")
    cols = lax.axis_size("col")
    tiles, own = left_blocks.shape[1], left_blocks.shape[2]
    block_rows = left_lengths.shape[2]
    sharing = peers // block_rows
    side = math.isqrt(left_blocks.shape[-1])
    height = block_rows * side

    def from_col(x, by):
        return x if by == 0 else lax.ppermute(x, "col", [(i, (i + by) % cols) for i in range(cols)])

    left, slots, lengths = left_blocks[0], left_slots[0], left_lengths[0]
    own_right = right_blocks[0, 0]

    if sharing == 2:
        bits = [1 << b for b in range(1, peers.bit_length() - 1)]
        zero = bits[-1:] + bits[:-1]
        one = bits[-1:] + bits[1:-1] + bits[:1]
        first = (zero[0], one[0])
        come = by_core(left, *first), by_core(slots, *first)
        stack = pack(left, slots, lengths, parts=2)
        sending, stack = lax.optimization_barrier((own_right, stack))
        sent = [from_col(sending, by) for by in range(1, cols)]
        stack = pack(come[0], come[1], lengths, first, parts=2, part=1, buffer=stack)
        held = [[stack], [swapped(stack, 1)]]
        for step, (a, b) in enumerate(zip(zero[1:-1], one[1:-1])):
            new = by_core(stack, a, b)
            rows = stack.shape[0]
            wide = fill(stack, 2 * rows)
            if step == 0:
                wide, places, count = lax.optimization_barrier((wide, right_places[0], right_count))
                spots = live_spots(places, count)
                places = [from_col(spots, by) for by in range(1, cols)]
                rights = [dense_right(own_right, spots, 13 * 10**8)]
                new, rights[0], sent, places = lax.optimization_barrier((new, rights[0], sent, places))
            held[0].append(new)
            held[1].append(swapped(new, 1))
            stack = fill(new, 2 * rows, rows, wide)
        rights += [dense_right(x, p) for x, p in zip(sent, places)]
        held[0].append(by_core(stack, zero[-1], one[-1]))
        final = len(held[0]) - 1

        def spread_at(order):
            found = {}
            for p, name in enumerate(spread(order)):
                part = max(p.bit_length() - 1, 0)
                found[name] = (part, p - (1 << part if part else 0))
            return found

        at_zero, at_one = spread_at(zero), spread_at(one)
        kinds = {}
        for name, (p, x) in at_zero.items():
            q, y = at_one[name]
            kinds.setdefault((p, q), []).append((name, x, y))

        def jobs(mine, theirs):
            zeros, ones = kinds.get((mine, theirs), []), kinds.get((theirs, mine), [])
            return [
                ((a, b), (mine, a_own, b_own), (theirs, a_other, b_other))
                for (a, a_own, a_other), (b, b_other, b_own) in zip(zeros, ones)
            ]

        early = range(final)
        groups = [
            [(p, q) for p in early for q in early],
            [(final, q) for q in early],
            [(p, final) for p in range(final + 1)],
        ]
        out = None
        for group in groups:
            arrays, keys, listed = [], {}, []

            def key(whose, part):
                if (whose, part) not in keys:
                    keys[whose, part] = len(arrays)
                    arrays.append(held[whose][part])
                return keys[whose, part]

            for mine, theirs in group:
                for masks, (m, x, y), (t, u, v) in jobs(mine, theirs):
                    listed.append((masks, [(key(0, m), x, y), (key(1, t), u, v)]))
            if listed:
                out = product(rights, arrays, listed, sharing, height, own // 2, out)
            if len(held[1]) == final:
                held[0][final], held[1], out = lax.optimization_barrier((held[0][final], held[1], out))
                held[1].append(swapped(held[0][final], 1))
        return out
    spots = live_spots(right_places[0], right_count)
    rights = [dense_right(from_col(own_right, by), from_col(spots, by)) for by in range(cols)]
    parcel = pack(left, slots, lengths)
    held = {0: parcel}
    for mask in range(4, peers, 4):
        held[mask] = swapped(parcel, mask)
    for mask in range(0, peers, 4):
        held[mask + 2] = swapped(held[mask], 2)
    for mask in range(0, peers, 2):
        held[mask + 1] = swapped(held[mask], 1)
    half = None
    for names in (range(peers // 2), range(peers // 2, peers)):
        listed = [
            ((names[i], names[i]), [(i + j, 0, 0) for j in range(sharing)]) for i in range(0, len(names), sharing)
        ]
        half = product(rights, [held[n] for n in names], listed, sharing, height, own // 2, half)
    return half


def solution(mesh):
    return jax.shard_map(
        shards,
        mesh=mesh,
        in_specs=(
            P("col", None, "row", None),
            P("col", None, "row"),
            P("col", None, None),
            P("col", "row", None, None),
            P("col", "row", None),
            P("col", "row"),
        ),
        out_specs=P("col", "row"),
        check_vma=False,
    )
```

```python
import functools
import math

import jax
import jax.numpy as jnp
from jax import lax
from jax.experimental import pallas as pl
from jax.experimental.pallas import tpu as pltpu
from jax.sharding import PartitionSpec as P

KB = 16
BCR = 16
LANES = 128
META = 16


def swapped(x, mask):
    peers = lax.axis_size("row")
    return lax.ppermute(x, "row", [(i, i ^ mask) for i in range(peers)])


def low_half(rows):
    return lax.broadcasted_iota(jnp.int32, (rows, LANES), 1) < LANES // 2


def pick_lane(row, at):
    lane = lax.broadcasted_iota(jnp.int32, row.shape, 1)
    return jnp.sum(jnp.where(lane == at, row, 0.0), axis=1, keepdims=True)


def pack_kernel(start, masks, slots_ref, lengths_ref, left_ref, *refs):
    out_ref, tall, square = refs[-3:]
    tiles, own, _ = left_ref.shape
    peers = lax.axis_size("row")
    me = lax.axis_index("row")
    mask = masks[0] if masks[0] == masks[1] else jnp.where(lax.rem(me, 2) == 0, masks[0], masks[1])
    per_row = peers * own // lengths_ref.shape[1]
    first = lax.bitwise_xor(me, mask) * own
    row = lax.div(first, per_row)
    place = lax.rem(first, per_row)
    group = lax.axis_index("col")
    low = low_half(32)
    low_meta = low_half(META)
    meta_row = lax.broadcasted_iota(jnp.int32, (META, LANES), 0)
    meta = jnp.full((META, LANES), -1.0, jnp.float32)
    at = 0
    for by in range(tiles):
        m = lax.rem(group - by + tiles, tiles)
        values = left_ref[m].astype(jnp.float32)
        for t in range(32):
            tall[pl.ds(by % 2 * 256 + t * 8, own), :] = values[:, t * LANES : (t + 1) * LANES]
        named = slots_ref[pl.ds(m, 1), :].astype(jnp.float32)
        live = pick_lane(lengths_ref[pl.ds(m, 1), :].astype(jnp.float32), row)
        for s in range(0, own, 2):
            one = tall[pl.ds(by % 2 * 256 + s, 32, stride=8), :]
            two = tall[pl.ds(by % 2 * 256 + s + 1, 32, stride=8), :]
            even = jnp.where(low, one, pltpu.roll(two, LANES // 2, 1))
            odd = jnp.where(low, pltpu.roll(one, LANES // 2, 1), two)
            y = square.at[at % 4]
            y[pl.ds(0, 32, stride=2), :] = even
            y[pl.ds(1, 32, stride=2), :] = odd
            out_ref[start + at * 64 : start + at * 64 + 64, :] = y[...].astype(out_ref.dtype)
            a = jnp.where((place + s).astype(jnp.float32) < live, pick_lane(named, s), -1.0)
            b = jnp.where((place + s + 1).astype(jnp.float32) < live, pick_lane(named, s + 1), -1.0)
            meta = jnp.where(meta_row == at, jnp.where(low_meta, a, b), meta)
            at += 1
    out_ref[start + at * 64 : start + at * 64 + META, :] = meta.astype(out_ref.dtype)


def pack(left, slots, lengths, masks=(0, 0), parts=1, part=0, buffer=None):
    tiles, own, _ = left.shape
    rows = tiles * own // 2 * 64 + META
    vmem = pl.BlockSpec(memory_space=pltpu.VMEM)
    given = [] if buffer is None else [buffer]
    return pl.pallas_call(
        functools.partial(pack_kernel, part * rows, masks),
        out_shape=jax.ShapeDtypeStruct((parts * rows, LANES), left.dtype),
        in_specs=[vmem] * (3 + len(given)),
        out_specs=vmem,
        scratch_shapes=[pltpu.VMEM((512, LANES), jnp.float32), pltpu.VMEM((4, 64, LANES), jnp.float32)],
        input_output_aliases={3: 0} if given else {},
        compiler_params=pltpu.CompilerParams(vmem_limit_bytes=4 * 1024 * 1024),
        cost_estimate=pl.CostEstimate(flops=3 * 10**8, bytes_accessed=1000, transcendentals=0),
    )(slots, lengths, left, *given)


def live_spots(places, count):
    slot = lax.broadcasted_iota(jnp.int32, places.shape, 1)
    return jnp.where(slot < count, places, -1)


def repeat(count, body):
    if count <= 2:
        for i in range(count):
            body(i)
    else:
        pl.loop(0, count)(body)


def right_kernel(places_ref, values_ref, dense_ref, tall, square):
    slots = values_ref.shape[0]
    half = lax.broadcasted_iota(jnp.int32, (32, LANES), 1) // (LANES // 2)
    dense_ref[...] = jnp.zeros_like(dense_ref)

    def some(g):
        values = values_ref[pl.ds(g * 16, 16), :].astype(jnp.float32)
        for t in range(32):
            tall[pl.ds(t * 16, 16), :] = values[:, t * LANES : (t + 1) * LANES]
        for s in range(16):
            spot = places_ref[0, g * 16 + s]
            live = spot >= 0
            spot = jnp.maximum(spot, 0)
            k, j = lax.shift_right_logical(spot, 4), lax.bitwise_and(spot, 15)
            side = lax.bitwise_and(j, 1)
            plain = tall[pl.ds(s, 32, stride=16), :]
            turned = pltpu.roll(plain, LANES // 2, 1)
            keep = half == jnp.where(live, side, -1)
            even = jnp.where(keep, jnp.where(side == 0, plain, turned), 0.0)
            odd = jnp.where(keep, jnp.where(side == 0, turned, plain), 0.0)
            y = square.at[s % square.shape[0]]
            y[pl.ds(0, 32, stride=2), :] = even
            y[pl.ds(1, 32, stride=2), :] = odd
            at = (
                pl.ds(pl.multiple_of(k * 64, 64), 64),
                pl.ds(pl.multiple_of(lax.shift_right_logical(j, 1) * LANES, LANES), LANES),
            )
            dense_ref[at] = dense_ref[at] + y[...].astype(dense_ref.dtype)

    repeat(slots // 16, some)


def dense_right(values, spots, work=0):
    side = math.isqrt(values.shape[1])
    smem, vmem = pl.BlockSpec(memory_space=pltpu.SMEM), pl.BlockSpec(memory_space=pltpu.VMEM)
    return pl.pallas_call(
        right_kernel,
        out_shape=jax.ShapeDtypeStruct((KB * side, BCR * side), values.dtype),
        in_specs=[smem, vmem],
        out_specs=vmem,
        scratch_shapes=[pltpu.VMEM((512, LANES), jnp.float32), pltpu.VMEM((4, side, LANES), jnp.float32)],
        compiler_params=pltpu.CompilerParams(vmem_limit_bytes=16 * 1024 * 1024),
        cost_estimate=pl.CostEstimate(flops=work, bytes_accessed=1000, transcendentals=0),
    )(spots, values)


def place_left(parcels, row, tiles, pairs, dense_ref, names_ref):
    half = (lax.broadcasted_iota(jnp.int32, (16, LANES), 1) // (LANES // 2)).astype(jnp.float32)
    body = tiles * pairs * 64
    for i, (parcel, start) in enumerate(parcels):
        names_ref[i * META : i * META + META, :] = parcel[pl.ds(start + body, META), :].astype(jnp.float32)

    def one(m):
        names = []
        for i, (parcel, start) in enumerate(parcels):
            for p in range(pairs):
                at = m * pairs + p
                name = jnp.broadcast_to(names_ref[pl.ds(i * META + at, 1), :], (16, LANES))
                turned = pltpu.roll(name, LANES // 2, 1)
                names.append((parcel, start + at * 64, (name - half).astype(jnp.bfloat16), (turned - half).astype(jnp.bfloat16)))
        plain, turned = [], []
        for parcel, start, _, _ in names:
            v = [parcel[pl.ds(start + c * 16, 16), :] for c in range(4)]
            plain.append(v)
            turned.append([pltpu.roll(x.astype(jnp.float32), LANES // 2, 1).astype(x.dtype) for x in v])
        for t in range(KB // 2):
            want = jnp.bfloat16(2 * t)
            hits = [(a == want, b == want) for _, _, a, b in names]
            for c in range(4):
                acc = jnp.zeros((16, LANES), dense_ref.dtype)
                for (a, b), v, w in zip(hits, plain, turned):
                    acc = jnp.where(a, v[c], acc)
                    acc = jnp.where(b, w[c], acc)
                dense_ref[
                    pl.ds(row * 64 + c * 16, 16),
                    pl.ds(pl.multiple_of(m * KB * 64 + t * LANES, LANES), LANES),
                ] = acc

    repeat(tiles, one)


def product_kernel(tiles, pairs, jobs, stacks, first_call, *refs):
    rights, refs = refs[:tiles], refs[tiles:]
    held, refs = refs[:stacks], refs[stacks:]
    if not first_call:
        refs = refs[1:]
    out_ref, left_dense, result, names, sems = refs
    sharing = names.shape[0] // META
    size = tiles * pairs * 64 + META
    me = lax.axis_index("row")
    core = lax.rem(me, 2)

    def pick(pair):
        return pair[0] if pair[0] == pair[1] else jnp.where(core == 0, pair[0], pair[1])

    for i, (_, parts) in enumerate(jobs):
        parcels = []
        for at, zero, one in parts:
            start = pick((zero * size, one * size))
            parcels.append((held[at], start if isinstance(start, int) else pl.multiple_of(start, 16)))
        place_left(parcels, i, tiles, pairs, left_dense, names)
    width = 256
    depth = rights[0].shape[0]
    copies = []
    for n in range(out_ref.shape[1] // width):
        span = slice(n * width, n * width + width)
        total = None
        for m in range(tiles):
            part = jnp.dot(
                left_dense[:, m * depth : m * depth + depth],
                rights[m][:, span],
                preferred_element_type=jnp.float32,
            )
            total = part if total is None else total + part
        result[:, span] = total
        if n % 2 == 1:
            wide = slice(n * width - width, n * width + width)
            for i, (masks, _) in enumerate(jobs):
                row = lax.div(lax.bitwise_xor(me, pick(masks)), sharing)
                copies.append(
                    pltpu.make_async_copy(
                        result.at[pl.ds(i * 64, 64), wide],
                        out_ref.at[pl.ds(pl.multiple_of(row * 64, 64), 64), wide],
                        sems.at[n // 2, i],
                    )
                )
                copies[-1].start()
    for copy in copies:
        copy.wait()


def product(rights, stacks, jobs, sharing, height, pairs, before=None):
    depth, width = rights[0].shape
    tiles, dtype = len(rights), rights[0].dtype
    rows = len(jobs) * 64
    vmem, hbm = pl.BlockSpec(memory_space=pltpu.VMEM), pl.BlockSpec(memory_space=pltpu.HBM)
    first = before is None
    return pl.pallas_call(
        functools.partial(product_kernel, tiles, pairs, jobs, len(stacks), first),
        out_shape=jax.ShapeDtypeStruct((height, width), jnp.float32),
        in_specs=[vmem] * (tiles + len(stacks)) + ([] if first else [hbm]),
        out_specs=hbm,
        scratch_shapes=[
            pltpu.VMEM((rows, tiles * depth), dtype),
            pltpu.VMEM((rows, width), jnp.float32),
            pltpu.VMEM((sharing * META, LANES), jnp.float32),
            pltpu.SemaphoreType.DMA((width // 512, len(jobs))),
        ],
        input_output_aliases={} if first else {tiles + len(stacks): 0},
        compiler_params=pltpu.CompilerParams(vmem_limit_bytes=(8 + 5 * tiles) * 1024 * 1024),
        cost_estimate=pl.CostEstimate(
            flops=10**6, bytes_accessed=1000, transcendentals=0
        ),
    )(*rights, *stacks, *([] if first else [before]))


def fill_kernel(start, part_ref, *refs):
    refs[-1][start : start + part_ref.shape[0], :] = part_ref[...]


def fill(part, rows, start=0, buffer=None):
    vmem = pl.BlockSpec(memory_space=pltpu.VMEM)
    given = [] if buffer is None else [buffer]
    return pl.pallas_call(
        functools.partial(fill_kernel, start),
        out_shape=jax.ShapeDtypeStruct((rows, LANES), part.dtype),
        in_specs=[vmem] * (1 + len(given)),
        out_specs=vmem,
        input_output_aliases={1: 0} if given else {},
        compiler_params=pltpu.CompilerParams(vmem_limit_bytes=4 * 1024 * 1024),
        cost_estimate=pl.CostEstimate(flops=1000000, bytes_accessed=1000, transcendentals=0),
    )(part, *given)


def by_core(x, zero, one):
    peers = lax.axis_size("row")
    return lax.ppermute(x, "row", [(i, i ^ (one if i % 2 else zero)) for i in range(peers)])


def spread(order):
    names = [0]
    for mask in order:
        names = names + [name ^ mask for name in names]
    return names


def shards(left_blocks, left_slots, left_lengths, right_blocks, right_places, right_count):
    peers = lax.axis_size("row")
    cols = lax.axis_size("col")
    tiles, own = left_blocks.shape[1], left_blocks.shape[2]
    block_rows = left_lengths.shape[2]
    sharing = peers // block_rows
    side = math.isqrt(left_blocks.shape[-1])
    height = block_rows * side

    def from_col(x, by):
        return x if by == 0 else lax.ppermute(x, "col", [(i, (i + by) % cols) for i in range(cols)])

    left, slots, lengths = left_blocks[0], left_slots[0], left_lengths[0]
    own_right = right_blocks[0, 0]

    if sharing == 2:
        bits = [1 << b for b in range(1, peers.bit_length() - 1)]
        zero = bits[-1:] + bits[:-1]
        one = bits[-1:] + bits[1:-1] + bits[:1]
        first = (zero[0], one[0])
        come = by_core(left, *first), by_core(slots, *first)
        stack = pack(left, slots, lengths, parts=2)
        sending, stack = lax.optimization_barrier((own_right, stack))
        sent = [from_col(sending, by) for by in range(1, cols)]
        stack = pack(come[0], come[1], lengths, first, parts=2, part=1, buffer=stack)
        held = [[stack], [swapped(stack, 1)]]
        for step, (a, b) in enumerate(zip(zero[1:-1], one[1:-1])):
            new = by_core(stack, a, b)
            rows = stack.shape[0]
            wide = fill(stack, 2 * rows)
            if step == 0:
                wide, places, count = lax.optimization_barrier((wide, right_places[0], right_count))
                spots = live_spots(places, count)
                places = [from_col(spots, by) for by in range(1, cols)]
                rights = [dense_right(own_right, spots, 13 * 10**8)]
                new, rights[0], sent, places = lax.optimization_barrier((new, rights[0], sent, places))
            held[0].append(new)
            held[1].append(swapped(new, 1))
            stack = fill(new, 2 * rows, rows, wide)
        rights += [dense_right(x, p) for x, p in zip(sent, places)]
        held[0].append(by_core(stack, zero[-1], one[-1]))
        final = len(held[0]) - 1

        def spread_at(order):
            found = {}
            for p, name in enumerate(spread(order)):
                part = max(p.bit_length() - 1, 0)
                found[name] = (part, p - (1 << part if part else 0))
            return found

        at_zero, at_one = spread_at(zero), spread_at(one)
        kinds = {}
        for name, (p, x) in at_zero.items():
            q, y = at_one[name]
            kinds.setdefault((p, q), []).append((name, x, y))

        def jobs(mine, theirs):
            zeros, ones = kinds.get((mine, theirs), []), kinds.get((theirs, mine), [])
            return [
                ((a, b), (mine, a_own, b_own), (theirs, a_other, b_other))
                for (a, a_own, a_other), (b, b_other, b_own) in zip(zeros, ones)
            ]

        early = range(final)
        groups = [
            [(p, q) for p in early for q in early],
            [(final, q) for q in early],
            [(p, final) for p in range(final + 1)],
        ]
        out = None
        for group in groups:
            arrays, keys, listed = [], {}, []

            def key(whose, part):
                if (whose, part) not in keys:
                    keys[whose, part] = len(arrays)
                    arrays.append(held[whose][part])
                return keys[whose, part]

            for mine, theirs in group:
                for masks, (m, x, y), (t, u, v) in jobs(mine, theirs):
                    listed.append((masks, [(key(0, m), x, y), (key(1, t), u, v)]))
            if listed:
                out = product(rights, arrays, listed, sharing, height, own // 2, out)
            if len(held[1]) == final:
                held[0][final], held[1], out = lax.optimization_barrier((held[0][final], held[1], out))
                held[1].append(swapped(held[0][final], 1))
        return out
    spots = live_spots(right_places[0], right_count)
    rights = [dense_right(from_col(own_right, by), from_col(spots, by)) for by in range(cols)]
    parcel = pack(left, slots, lengths)
    held = {0: parcel}
    for mask in range(4, peers, 4):
        held[mask] = swapped(parcel, mask)
    for mask in range(0, peers, 4):
        held[mask + 2] = swapped(held[mask], 2)
    for mask in range(0, peers, 2):
        held[mask + 1] = swapped(held[mask], 1)
    half = None
    for names in (range(peers // 2), range(peers // 2, peers)):
        listed = [
            ((names[i], names[i]), [(i + j, 0, 0) for j in range(sharing)]) for i in range(0, len(names), sharing)
        ]
        half = product(rights, [held[n] for n in names], listed, sharing, height, own // 2, half)
    return half


def solution(mesh):
    return jax.shard_map(
        shards,
        mesh=mesh,
        in_specs=(
            P("col", None, "row", None),
            P("col", None, "row"),
            P("col", None, None),
            P("col", "row", None, None),
            P("col", "row", None),
            P("col", "row"),
        ),
        out_specs=P("col", "row"),
        check_vma=False,
    )
```

```python
import functools
import math

import jax
import jax.numpy as jnp
from jax import lax
from jax.experimental import pallas as pl
from jax.experimental.pallas import tpu as pltpu
from jax.sharding import PartitionSpec as P

KB = 16
BCR = 16
LANES = 128
META = 16


def swapped(x, mask):
    peers = lax.axis_size("row")
    return lax.ppermute(x, "row", [(i, i ^ mask) for i in range(peers)])


def low_half(rows):
    return lax.broadcasted_iota(jnp.int32, (rows, LANES), 1) < LANES // 2


def pick_lane(row, at):
    lane = lax.broadcasted_iota(jnp.int32, row.shape, 1)
    return jnp.sum(jnp.where(lane == at, row, 0.0), axis=1, keepdims=True)


def pack_kernel(start, masks, slots_ref, lengths_ref, left_ref, *refs):
    out_ref, tall, square = refs[-3:]
    tiles, own, _ = left_ref.shape
    peers = lax.axis_size("row")
    me = lax.axis_index("row")
    mask = masks[0] if masks[0] == masks[1] else jnp.where(lax.rem(me, 2) == 0, masks[0], masks[1])
    per_row = peers * own // lengths_ref.shape[1]
    first = lax.bitwise_xor(me, mask) * own
    row = lax.div(first, per_row)
    place = lax.rem(first, per_row)
    group = lax.axis_index("col")
    low = low_half(32)
    low_meta = low_half(META)
    meta_row = lax.broadcasted_iota(jnp.int32, (META, LANES), 0)
    meta = jnp.full((META, LANES), -1.0, jnp.float32)
    at = 0
    for by in range(tiles):
        m = lax.rem(group - by + tiles, tiles)
        values = left_ref[m].astype(jnp.float32)
        for t in range(32):
            tall[pl.ds(by % 2 * 256 + t * 8, own), :] = values[:, t * LANES : (t + 1) * LANES]
        named = slots_ref[pl.ds(m, 1), :].astype(jnp.float32)
        live = pick_lane(lengths_ref[pl.ds(m, 1), :].astype(jnp.float32), row)
        for s in range(0, own, 2):
            one = tall[pl.ds(by % 2 * 256 + s, 32, stride=8), :]
            two = tall[pl.ds(by % 2 * 256 + s + 1, 32, stride=8), :]
            even = jnp.where(low, one, pltpu.roll(two, LANES // 2, 1))
            odd = jnp.where(low, pltpu.roll(one, LANES // 2, 1), two)
            y = square.at[at % 4]
            y[pl.ds(0, 32, stride=2), :] = even
            y[pl.ds(1, 32, stride=2), :] = odd
            out_ref[start + at * 64 : start + at * 64 + 64, :] = y[...].astype(out_ref.dtype)
            a = jnp.where((place + s).astype(jnp.float32) < live, pick_lane(named, s), -1.0)
            b = jnp.where((place + s + 1).astype(jnp.float32) < live, pick_lane(named, s + 1), -1.0)
            meta = jnp.where(meta_row == at, jnp.where(low_meta, a, b), meta)
            at += 1
    out_ref[start + at * 64 : start + at * 64 + META, :] = meta.astype(out_ref.dtype)


def pack(left, slots, lengths, masks=(0, 0), parts=1, part=0, buffer=None):
    tiles, own, _ = left.shape
    rows = tiles * own // 2 * 64 + META
    vmem = pl.BlockSpec(memory_space=pltpu.VMEM)
    given = [] if buffer is None else [buffer]
    return pl.pallas_call(
        functools.partial(pack_kernel, part * rows, masks),
        out_shape=jax.ShapeDtypeStruct((parts * rows, LANES), left.dtype),
        in_specs=[vmem] * (3 + len(given)),
        out_specs=vmem,
        scratch_shapes=[pltpu.VMEM((512, LANES), jnp.float32), pltpu.VMEM((4, 64, LANES), jnp.float32)],
        input_output_aliases={3: 0} if given else {},
        compiler_params=pltpu.CompilerParams(vmem_limit_bytes=4 * 1024 * 1024),
        cost_estimate=pl.CostEstimate(flops=3 * 10**8, bytes_accessed=1000, transcendentals=0),
    )(slots, lengths, left, *given)


def live_spots(places, count):
    slot = lax.broadcasted_iota(jnp.int32, places.shape, 1)
    return jnp.where(slot < count, places, -1)


def repeat(count, body):
    if count <= 2:
        for i in range(count):
            body(i)
    else:
        pl.loop(0, count)(body)


def right_kernel(places_ref, values_ref, dense_ref, tall, square):
    slots = values_ref.shape[0]
    half = lax.broadcasted_iota(jnp.int32, (32, LANES), 1) // (LANES // 2)
    dense_ref[...] = jnp.zeros_like(dense_ref)

    def some(g):
        values = values_ref[pl.ds(g * 16, 16), :].astype(jnp.float32)
        for t in range(32):
            tall[pl.ds(t * 16, 16), :] = values[:, t * LANES : (t + 1) * LANES]
        for s in range(16):
            spot = places_ref[0, g * 16 + s]
            live = spot >= 0
            spot = jnp.maximum(spot, 0)
            k, j = lax.shift_right_logical(spot, 4), lax.bitwise_and(spot, 15)
            side = lax.bitwise_and(j, 1)
            plain = tall[pl.ds(s, 32, stride=16), :]
            turned = pltpu.roll(plain, LANES // 2, 1)
            keep = half == jnp.where(live, side, -1)
            even = jnp.where(keep, jnp.where(side == 0, plain, turned), 0.0)
            odd = jnp.where(keep, jnp.where(side == 0, turned, plain), 0.0)
            y = square.at[s % square.shape[0]]
            y[pl.ds(0, 32, stride=2), :] = even
            y[pl.ds(1, 32, stride=2), :] = odd
            at = (
                pl.ds(pl.multiple_of(k * 64, 64), 64),
                pl.ds(pl.multiple_of(lax.shift_right_logical(j, 1) * LANES, LANES), LANES),
            )
            dense_ref[at] = dense_ref[at] + y[...].astype(dense_ref.dtype)

    repeat(slots // 16, some)


def dense_right(values, spots, work=0):
    side = math.isqrt(values.shape[1])
    smem, vmem = pl.BlockSpec(memory_space=pltpu.SMEM), pl.BlockSpec(memory_space=pltpu.VMEM)
    return pl.pallas_call(
        right_kernel,
        out_shape=jax.ShapeDtypeStruct((KB * side, BCR * side), values.dtype),
        in_specs=[smem, vmem],
        out_specs=vmem,
        scratch_shapes=[pltpu.VMEM((512, LANES), jnp.float32), pltpu.VMEM((4, side, LANES), jnp.float32)],
        compiler_params=pltpu.CompilerParams(vmem_limit_bytes=16 * 1024 * 1024),
        cost_estimate=pl.CostEstimate(flops=work, bytes_accessed=1000, transcendentals=0),
    )(spots, values)


def place_left(parcels, row, tiles, pairs, dense_ref, names_ref):
    half = (lax.broadcasted_iota(jnp.int32, (16, LANES), 1) // (LANES // 2)).astype(jnp.float32)
    body = tiles * pairs * 64
    rows = [parcel[pl.ds(start + body, META), :].astype(jnp.float32) for parcel, start in parcels]
    if tiles > 2:
        for i, row_names in enumerate(rows):
            names_ref[i * META : i * META + META, :] = row_names

    def one(m):
        names = []
        for i, (parcel, start) in enumerate(parcels):
            for p in range(pairs):
                at = m * pairs + p
                name = names_ref[pl.ds(i * META + at, 1), :] if tiles > 2 else rows[i][at : at + 1, :]
                name = jnp.broadcast_to(name, (16, LANES))
                turned = pltpu.roll(name, LANES // 2, 1)
                names.append((parcel, start + at * 64, (name - half).astype(jnp.bfloat16), (turned - half).astype(jnp.bfloat16)))
        plain, turned = [], []
        for parcel, start, _, _ in names:
            v = [parcel[pl.ds(start + c * 16, 16), :] for c in range(4)]
            plain.append(v)
            turned.append([pltpu.roll(x.astype(jnp.float32), LANES // 2, 1).astype(x.dtype) for x in v])
        for t in range(KB // 2):
            want = jnp.bfloat16(2 * t)
            hits = [(a == want, b == want) for _, _, a, b in names]
            for c in range(4):
                acc = jnp.zeros((16, LANES), dense_ref.dtype)
                for (a, b), v, w in zip(hits, plain, turned):
                    acc = jnp.where(a, v[c], acc)
                    acc = jnp.where(b, w[c], acc)
                dense_ref[
                    pl.ds(row * 64 + c * 16, 16),
                    pl.ds(pl.multiple_of(m * KB * 64 + t * LANES, LANES), LANES),
                ] = acc

    repeat(tiles, one)


def product_kernel(tiles, pairs, jobs, stacks, first_call, *refs):
    rights, refs = refs[:tiles], refs[tiles:]
    held, refs = refs[:stacks], refs[stacks:]
    if not first_call:
        refs = refs[1:]
    out_ref, left_dense, result, names, sems = refs
    sharing = names.shape[0] // META
    size = tiles * pairs * 64 + META
    me = lax.axis_index("row")
    core = lax.rem(me, 2)

    def pick(pair):
        return pair[0] if pair[0] == pair[1] else jnp.where(core == 0, pair[0], pair[1])

    for i, (_, parts) in enumerate(jobs):
        parcels = []
        for at, zero, one in parts:
            start = pick((zero * size, one * size))
            parcels.append((held[at], start if isinstance(start, int) else pl.multiple_of(start, 16)))
        place_left(parcels, i, tiles, pairs, left_dense, names)
    width = 256
    depth = rights[0].shape[0]
    copies = []
    for n in range(out_ref.shape[1] // width):
        span = slice(n * width, n * width + width)
        total = None
        for m in range(tiles):
            part = jnp.dot(
                left_dense[:, m * depth : m * depth + depth],
                rights[m][:, span],
                preferred_element_type=jnp.float32,
            )
            total = part if total is None else total + part
        result[:, span] = total
        if n % 2 == 1:
            wide = slice(n * width - width, n * width + width)
            for i, (masks, _) in enumerate(jobs):
                row = lax.div(lax.bitwise_xor(me, pick(masks)), sharing)
                copies.append(
                    pltpu.make_async_copy(
                        result.at[pl.ds(i * 64, 64), wide],
                        out_ref.at[pl.ds(pl.multiple_of(row * 64, 64), 64), wide],
                        sems.at[n // 2, i],
                    )
                )
                copies[-1].start()
    for copy in copies:
        copy.wait()


def product(rights, stacks, jobs, sharing, height, pairs, before=None):
    depth, width = rights[0].shape
    tiles, dtype = len(rights), rights[0].dtype
    rows = len(jobs) * 64
    vmem, hbm = pl.BlockSpec(memory_space=pltpu.VMEM), pl.BlockSpec(memory_space=pltpu.HBM)
    first = before is None
    return pl.pallas_call(
        functools.partial(product_kernel, tiles, pairs, jobs, len(stacks), first),
        out_shape=jax.ShapeDtypeStruct((height, width), jnp.float32),
        in_specs=[vmem] * (tiles + len(stacks)) + ([] if first else [hbm]),
        out_specs=hbm,
        scratch_shapes=[
            pltpu.VMEM((rows, tiles * depth), dtype),
            pltpu.VMEM((rows, width), jnp.float32),
            pltpu.VMEM((sharing * META, LANES), jnp.float32),
            pltpu.SemaphoreType.DMA((width // 512, len(jobs))),
        ],
        input_output_aliases={} if first else {tiles + len(stacks): 0},
        compiler_params=pltpu.CompilerParams(vmem_limit_bytes=(8 + 5 * tiles) * 1024 * 1024),
        cost_estimate=pl.CostEstimate(
            flops=10**6, bytes_accessed=1000, transcendentals=0
        ),
    )(*rights, *stacks, *([] if first else [before]))


def fill_kernel(start, part_ref, *refs):
    refs[-1][start : start + part_ref.shape[0], :] = part_ref[...]


def fill(part, rows, start=0, buffer=None):
    vmem = pl.BlockSpec(memory_space=pltpu.VMEM)
    given = [] if buffer is None else [buffer]
    return pl.pallas_call(
        functools.partial(fill_kernel, start),
        out_shape=jax.ShapeDtypeStruct((rows, LANES), part.dtype),
        in_specs=[vmem] * (1 + len(given)),
        out_specs=vmem,
        input_output_aliases={1: 0} if given else {},
        compiler_params=pltpu.CompilerParams(vmem_limit_bytes=4 * 1024 * 1024),
        cost_estimate=pl.CostEstimate(flops=1000000, bytes_accessed=1000, transcendentals=0),
    )(part, *given)


def by_core(x, zero, one):
    peers = lax.axis_size("row")
    return lax.ppermute(x, "row", [(i, i ^ (one if i % 2 else zero)) for i in range(peers)])


def spread(order):
    names = [0]
    for mask in order:
        names = names + [name ^ mask for name in names]
    return names


def shards(left_blocks, left_slots, left_lengths, right_blocks, right_places, right_count):
    peers = lax.axis_size("row")
    cols = lax.axis_size("col")
    tiles, own = left_blocks.shape[1], left_blocks.shape[2]
    block_rows = left_lengths.shape[2]
    sharing = peers // block_rows
    side = math.isqrt(left_blocks.shape[-1])
    height = block_rows * side

    def from_col(x, by):
        return x if by == 0 else lax.ppermute(x, "col", [(i, (i + by) % cols) for i in range(cols)])

    left, slots, lengths = left_blocks[0], left_slots[0], left_lengths[0]
    own_right = right_blocks[0, 0]

    if sharing == 2:
        bits = [1 << b for b in range(1, peers.bit_length() - 1)]
        zero = bits[-1:] + bits[:-1]
        one = bits[-1:] + bits[1:-1] + bits[:1]
        first = (zero[0], one[0])
        come = by_core(left, *first), by_core(slots, *first)
        stack = pack(left, slots, lengths, parts=2)
        sending, stack = lax.optimization_barrier((own_right, stack))
        sent = [from_col(sending, by) for by in range(1, cols)]
        stack = pack(come[0], come[1], lengths, first, parts=2, part=1, buffer=stack)
        held = [[stack], [swapped(stack, 1)]]
        for step, (a, b) in enumerate(zip(zero[1:-1], one[1:-1])):
            new = by_core(stack, a, b)
            rows = stack.shape[0]
            wide = fill(stack, 2 * rows)
            if step == 0:
                wide, places, count = lax.optimization_barrier((wide, right_places[0], right_count))
                spots = live_spots(places, count)
                places = [from_col(spots, by) for by in range(1, cols)]
                rights = [dense_right(own_right, spots, 13 * 10**8)]
                new, rights[0], sent, places = lax.optimization_barrier((new, rights[0], sent, places))
            held[0].append(new)
            held[1].append(swapped(new, 1))
            stack = fill(new, 2 * rows, rows, wide)
        rights += [dense_right(x, p) for x, p in zip(sent, places)]
        held[0].append(by_core(stack, zero[-1], one[-1]))
        final = len(held[0]) - 1

        def spread_at(order):
            found = {}
            for p, name in enumerate(spread(order)):
                part = max(p.bit_length() - 1, 0)
                found[name] = (part, p - (1 << part if part else 0))
            return found

        at_zero, at_one = spread_at(zero), spread_at(one)
        kinds = {}
        for name, (p, x) in at_zero.items():
            q, y = at_one[name]
            kinds.setdefault((p, q), []).append((name, x, y))

        def jobs(mine, theirs):
            zeros, ones = kinds.get((mine, theirs), []), kinds.get((theirs, mine), [])
            return [
                ((a, b), (mine, a_own, b_own), (theirs, a_other, b_other))
                for (a, a_own, a_other), (b, b_other, b_own) in zip(zeros, ones)
            ]

        early = range(final)
        groups = [
            [(p, q) for p in early for q in early],
            [(final, q) for q in early],
            [(p, final) for p in range(final + 1)],
        ]
        out = None
        for group in groups:
            arrays, keys, listed = [], {}, []

            def key(whose, part):
                if (whose, part) not in keys:
                    keys[whose, part] = len(arrays)
                    arrays.append(held[whose][part])
                return keys[whose, part]

            for mine, theirs in group:
                for masks, (m, x, y), (t, u, v) in jobs(mine, theirs):
                    listed.append((masks, [(key(0, m), x, y), (key(1, t), u, v)]))
            if listed:
                out = product(rights, arrays, listed, sharing, height, own // 2, out)
            if len(held[1]) == final:
                held[0][final], held[1], out = lax.optimization_barrier((held[0][final], held[1], out))
                held[1].append(swapped(held[0][final], 1))
        return out
    spots = live_spots(right_places[0], right_count)
    rights = [dense_right(from_col(own_right, by), from_col(spots, by)) for by in range(cols)]
    parcel = pack(left, slots, lengths)
    held = {0: parcel}
    for mask in range(4, peers, 4):
        held[mask] = swapped(parcel, mask)
    for mask in range(0, peers, 4):
        held[mask + 2] = swapped(held[mask], 2)
    for mask in range(0, peers, 2):
        held[mask + 1] = swapped(held[mask], 1)
    half = None
    for names in (range(peers // 2), range(peers // 2, peers)):
        listed = [
            ((names[i], names[i]), [(i + j, 0, 0) for j in range(sharing)]) for i in range(0, len(names), sharing)
        ]
        half = product(rights, [held[n] for n in names], listed, sharing, height, own // 2, half)
    return half


def solution(mesh):
    return jax.shard_map(
        shards,
        mesh=mesh,
        in_specs=(
            P("col", None, "row", None),
            P("col", None, "row"),
            P("col", None, None),
            P("col", "row", None, None),
            P("col", "row", None),
            P("col", "row"),
        ),
        out_specs=P("col", "row"),
        check_vma=False,
    )
```
